32 devices in a mesh: expert: 8 (over z, y), hidden: 4 (over x, core).
Axes of the slice: x: 2, y: 2, z: 4, core: 2. Of those that a mesh axis runs over, the one named last changes fastest.
Arguments:
- tokens: bfloat16 [4096, 2048], P(('expert', 'hidden')), may hold values from -6 to 6
- grad_out: bfloat16 [4096, 2048], P(('expert', 'hidden')), may hold values from -6 to 6
- picks: int32 [16, 512], P('expert'), may hold values from 0 to 4095, as said below
- gates: float32 [16, 512], P('expert'), may hold values from 0.1 to 1
- w_gate: bfloat16 [16, 768, 2048], P('expert', 'hidden'), may hold values from -0.125 to 0.125
- w_up: bfloat16 [16, 768, 2048], P('expert', 'hidden'), may hold values from -0.125 to 0.125
- w_down: bfloat16 [16, 768, 2048], P('expert', 'hidden'), may hold values from -0.21875 to 0.21875
Outputs:
- grad_tokens: bfloat16 [4096, 2048], P(('expert', 'hidden'))
- grad_scores: float32 [16, 512], P('expert')
- grad_w_gate: bfloat16 [16, 768, 2048], P('expert', 'hidden')
- grad_w_up: bfloat16 [16, 768, 2048], P('expert', 'hidden')
- grad_w_down: bfloat16 [16, 768, 2048], P('expert', 'hidden')
The draws below stay inside these ranges and needn't reach their ends.
Inputs may be any that keep to these rules, and one draw needn't show every extreme that they name: Each row lists 512 different token indices in ascending order. For every expert at most 32 of its picks lie in one aligned block of 128 tokens, and some block holds exactly 32.
All inputs are finite; a program needn't handle non-finite values.
Results may differ from the reference program's by a relative error of at most 0.01.
Values may be sent and summed in bfloat16 or wider, within the bound.
A program may use at most 128 MiB of HBM per device.

```python
import math
import jax
import jax.numpy as jnp
from jax import lax

D = 2048
HID = 768
TOK_DEV = 128
EXPERTS = 16
TOKENS = 4096
CAP = 512
HIDS = 192
PEER_MOST = 32
N_HIDDEN = 4


def draw_picks(key, part):
    key = jax.random.fold_in(key, 11)
    owners = TOKENS // TOK_DEV
    key_order, key_rank, key_forced = jax.random.split(key, 3)
    bits = jax.random.randint(key_order, (EXPERTS, owners, TOK_DEV), 0, 4096)
    scores = bits * TOK_DEV + jnp.arange(TOK_DEV, dtype=jnp.int32)[None, None, :]
    order = jnp.argsort(scores, axis=-1)[:, :, :PEER_MOST].astype(jnp.int32)
    candidates = order + (jnp.arange(owners, dtype=jnp.int32) * TOK_DEV)[None, :, None]
    candidates = candidates.reshape(EXPERTS, owners * PEER_MOST)
    total = owners * PEER_MOST
    ranks = jax.random.randint(key_rank, (EXPERTS, total), 0, 4096) * total + jnp.arange(total, dtype=jnp.int32)[None, :]
    forced = jax.random.randint(key_forced, (EXPERTS, 1), 0, owners)
    owner_of = (jnp.arange(total, dtype=jnp.int32) // PEER_MOST)[None, :]
    keys_all = jnp.where(owner_of == forced, 0, 1 << 28) + ranks
    chosen_pos = jnp.argsort(keys_all, axis=-1)[:, :CAP]
    chosen = jnp.take_along_axis(candidates, chosen_pos, axis=-1)
    return jnp.sort(chosen, axis=-1).astype(jnp.int32)


def block_scale(own_key, dims, cuts, smallest, high):
    factor_of, own = 1.0, jax.random.fold_in(own_key, 6)
    for dim, blocks in cuts:
        draws = jnp.exp(jax.random.uniform(jax.random.fold_in(own, dim), (blocks,), jnp.float32, smallest / len(cuts), high / len(cuts)))
        factor_of = factor_of * jnp.repeat(draws, dims[dim] // blocks).reshape([-1 if axis == dim else 1 for axis in range(len(dims))])
    return factor_of


def bell_draw(key, shape, width, limit, cuts=(), kind=jnp.bfloat16):
    array = width * jax.random.normal(key, shape, jnp.float32)
    if cuts:
        array = array * block_scale(key, shape, cuts, -0.22, 0.18)
    return jnp.clip(array, -limit, limit).astype(kind)


def setup_inputs(seed: int = 0) -> dict:
    keys = jax.random.split(jax.random.key(seed), 8)
    tokens = bell_draw(keys[0], (TOKENS, D), 1.0, 6.0, ((0, 32),))
    grad_out = bell_draw(keys[1], (TOKENS, D), 1.0, 6.0, ((0, 32),))
    picks = draw_picks(jax.random.fold_in(keys[7], 71), 0)
    gates = jnp.clip(jnp.exp(math.log(1.0) - 2.3025851 * jax.random.uniform(keys[3], (EXPERTS, CAP), jnp.float32) ** block_scale(keys[3], (EXPERTS, CAP), ((0, 8),), -0.2, 0.2)), 0.1, 1.0)
    w_gate = bell_draw(keys[4], (EXPERTS, HID, D), D ** -0.5, 0.125, ((0, 8), (1, 4)))
    w_up = bell_draw(keys[5], (EXPERTS, HID, D), D ** -0.5, 0.125, ((0, 8), (1, 4)))
    w_down = bell_draw(keys[6], (EXPERTS, HID, D), HID ** -0.5, 0.21875, ((0, 8), (1, 4)))
    return {"tokens": tokens, "grad_out": grad_out, "picks": picks, "gates": gates, "w_gate": w_gate, "w_up": w_up, "w_down": w_down}


def expert_backward(args, tokens, grad_out):
    rows_idx, gate_w, wg, wu, wd = args
    picked = tokens[rows_idx]
    picked_grad = grad_out[rows_idx]
    gate = jnp.dot(picked, wg.T, preferred_element_type=jnp.float32)
    up = jnp.dot(picked, wu.T, preferred_element_type=jnp.float32)
    sig = jax.nn.sigmoid(gate)
    act = gate * sig
    hid = (act * up).astype(jnp.bfloat16)
    back = jnp.dot(picked_grad, wd.T, preferred_element_type=jnp.float32)
    score = jnp.sum(hid.astype(jnp.float32) * back, axis=-1)
    grad_hid = gate_w[:, None] * back
    grad_gate = (grad_hid * up * sig * (1.0 + gate * (1.0 - sig))).astype(jnp.bfloat16)
    grad_up = (grad_hid * act).astype(jnp.bfloat16)
    weighted = (gate_w[:, None] * hid.astype(jnp.float32)).astype(jnp.bfloat16)
    gw_down = jnp.dot(weighted.T, picked_grad, preferred_element_type=jnp.float32).astype(jnp.bfloat16)
    gw_gate = jnp.dot(grad_gate.T, picked, preferred_element_type=jnp.float32).astype(jnp.bfloat16)
    gw_up = jnp.dot(grad_up.T, picked, preferred_element_type=jnp.float32).astype(jnp.bfloat16)
    gate_blocks = grad_gate.reshape(CAP, N_HIDDEN, HIDS).astype(jnp.float32)
    up_blocks = grad_up.reshape(CAP, N_HIDDEN, HIDS).astype(jnp.float32)
    wg_blocks = wg.reshape(N_HIDDEN, HIDS, D).astype(jnp.float32)
    wu_blocks = wu.reshape(N_HIDDEN, HIDS, D).astype(jnp.float32)
    parts = jnp.einsum("cbh,bhd->bcd", gate_blocks, wg_blocks) + jnp.einsum("cbh,bhd->bcd", up_blocks, wu_blocks)
    rounded = lax.optimization_barrier(parts.astype(jnp.bfloat16))
    rows_grad = jnp.sum(rounded.astype(jnp.float32), axis=0).astype(jnp.bfloat16)
    return rows_grad, score, gw_gate, gw_up, gw_down


def reference(tokens, grad_out, picks, gates, w_gate, w_up, w_down):
    rows_grad, grad_scores, grad_w_gate, grad_w_up, grad_w_down = lax.map(
        lambda args: expert_backward(args, tokens, grad_out), (picks, gates, w_gate, w_up, w_down))
    summed = jnp.zeros((TOKENS, D), jnp.float32).at[picks.reshape(-1)].add(
        rows_grad.reshape(-1, D).astype(jnp.float32))
    return summed.astype(jnp.bfloat16), grad_scores, grad_w_gate, grad_w_up, grad_w_down
```

```python
import jax
import jax.numpy as jnp
from jax import lax
from jax.sharding import PartitionSpec as P


def local(tokens, grad_out, picks, gates, w_gate, w_up, w_down):
    groups = lax.axis_size("expert")
    shares = lax.axis_size("hidden")
    tok_rows, width = tokens.shape
    exp_local, capacity = picks.shape
    total = groups * shares * tok_rows
    cols = width // shares
    flat = picks.reshape(-1)

    def spread(rows):
        part = lax.all_to_all(rows, "hidden", split_axis=1, concat_axis=0, tiled=True)
        return lax.all_gather(part, "expert", axis=0, tiled=True)

    def collect(everything):
        mine = everything[flat]
        return lax.all_gather(mine, "hidden", axis=1, tiled=True).reshape(exp_local, capacity, width)

    picked_grad = collect(spread(grad_out))
    picked = collect(spread(tokens))
    back = jnp.einsum("xcd,xhd->xch", picked_grad, w_down, preferred_element_type=jnp.float32)
    gate = jnp.einsum("xcd,xhd->xch", picked, w_gate, preferred_element_type=jnp.float32)
    up = jnp.einsum("xcd,xhd->xch", picked, w_up, preferred_element_type=jnp.float32)
    sig = jax.nn.sigmoid(gate)
    act = gate * sig
    hid = (act * up).astype(jnp.bfloat16)
    score_part = jnp.sum(hid.astype(jnp.float32) * back, axis=-1)
    grad_scores = lax.psum(score_part, "hidden")
    grad_hid = gates[:, :, None] * back
    grad_gate = (grad_hid * up * sig * (1.0 + gate * (1.0 - sig))).astype(jnp.bfloat16)
    grad_up = (grad_hid * act).astype(jnp.bfloat16)
    weighted = (gates[:, :, None] * hid.astype(jnp.float32)).astype(jnp.bfloat16)
    partial_rows = (
        jnp.einsum("xch,xhd->xcd", grad_gate, w_gate, preferred_element_type=jnp.float32)
        + jnp.einsum("xch,xhd->xcd", grad_up, w_up, preferred_element_type=jnp.float32)
    ).astype(jnp.bfloat16)
    rows_grad = lax.psum_scatter(
        partial_rows.reshape(exp_local * capacity, width), "hidden", scatter_dimension=1, tiled=True
    )
    selector = (jnp.arange(total, dtype=jnp.int32)[:, None] == flat[None, :]).astype(jnp.bfloat16)
    sums = jnp.dot(selector, rows_grad, preferred_element_type=jnp.float32).astype(jnp.bfloat16)
    own = lax.psum_scatter(sums, "expert", scatter_dimension=0, tiled=True)
    grad_tokens = lax.all_to_all(own, "hidden", split_axis=0, concat_axis=1, tiled=True)
    grad_w_down = jnp.einsum(
        "xch,xcd->xhd", weighted, picked_grad, preferred_element_type=jnp.float32
    ).astype(jnp.bfloat16)
    grad_w_gate = jnp.einsum(
        "xch,xcd->xhd", grad_gate, picked, preferred_element_type=jnp.float32
    ).astype(jnp.bfloat16)
    grad_w_up = jnp.einsum(
        "xch,xcd->xhd", grad_up, picked, preferred_element_type=jnp.float32
    ).astype(jnp.bfloat16)
    return (grad_tokens, grad_scores, grad_w_gate, grad_w_up, grad_w_down)


def solution(mesh):
    placed = (
        P(("expert", "hidden"), None),
        P(("expert", "hidden"), None),
        P("expert", None),
        P("expert", None),
        P("expert", "hidden", None),
        P("expert", "hidden", None),
        P("expert", "hidden", None),
    )
    return jax.shard_map(
        local,
        mesh=mesh,
        in_specs=placed,
        out_specs=(
            P(("expert", "hidden"), None),
            P("expert", None),
            P("expert", "hidden", None),
            P("expert", "hidden", None),
            P("expert", "hidden", None),
        ),
        check_vma=False,
    )
```

```python
import functools
import jax
import jax.numpy as jnp
from jax import lax
from jax.experimental import pallas as pl
from jax.experimental.pallas import tpu as pltpu
from jax.sharding import PartitionSpec as P

MESH = pl.DeviceIdType.MESH
PASSES = 4


def dispatch_kernel(
    nz, tok_ref, grad_ref, picks_ref, out_tok, out_grad, buf, hot,
    a_send, a_recv, up_send, up_recv, dn_send, dn_recv, y_send, y_recv,
    x_send, x_recv, c_send, c_recv,
):
    e, h = lax.axis_index("expert"), lax.axis_index("hidden")
    z, y = e // 2, e % 2
    h_core = h + 1 - 2 * (h % 2)
    h_x = (h + 2) % 4
    h_far = (h_core + 2) % 4
    rows, width = tok_ref.shape
    cols = width // 4
    part = buf.shape[-1]
    halves = cols // part
    peers = (h_core, h_x, h_far)
    groups = 2 * nz
    block = 4 * rows

    barrier = pltpu.get_barrier_semaphore()
    for peer in peers:
        pl.semaphore_signal(barrier, inc=1, device_id=(e, peer), device_id_type=MESH)
    pl.semaphore_signal(barrier, inc=1, device_id=(z * 2 + 1 - y, h), device_id_type=MESH)

    @pl.when(z > 0)
    def _():
        pl.semaphore_signal(barrier, inc=1, device_id=(e - 2, h), device_id_type=MESH)

    @pl.when(z < nz - 1)
    def _():
        pl.semaphore_signal(barrier, inc=1, device_id=(e + 2, h), device_id_type=MESH)

    ends = jnp.where(z == 0, 1, 0) + jnp.where(z == nz - 1, 1, 0)
    pl.semaphore_wait(barrier, 6 - ends)

    def source(p):
        return (tok_ref, grad_ref)[p // halves]

    def output(p):
        return (out_tok, out_grad)[p // halves]

    def span(p, owner):
        return pl.ds(pl.multiple_of(owner * cols + (p % halves) * part, part), part)

    def mine(p):
        return buf.at[p, e, pl.ds(pl.multiple_of(h * rows, rows), rows), :]

    def a_copy(p, d):
        return pltpu.make_async_remote_copy(
            src_ref=source(p).at[:, span(p, peers[d])], dst_ref=mine(p),
            send_sem=a_send.at[p, d], recv_sem=a_recv.at[p, d],
            device_id=(e, peers[d]), device_id_type=MESH)

    def chunk_copy(p, zz, send, recv, target):
        ref = buf.at[p, zz * 2 + y]
        return pltpu.make_async_remote_copy(
            src_ref=ref, dst_ref=ref, send_sem=send, recv_sem=recv,
            device_id=(target, h), device_id_type=MESH)

    def up(p, s):
        return chunk_copy(p, z - (s - 1), up_send.at[p, s - 1], up_recv.at[p, s - 1], e + 2)

    def dn(p, s):
        return chunk_copy(p, z + (s - 1), dn_send.at[p, s - 1], dn_recv.at[p, s - 1], e - 2)

    def across(p, k, zz):
        return chunk_copy(p, zz, y_send.at[p, k], y_recv.at[p, k], z * 2 + 1 - y)

    def x_copy(p):
        ref = output(p).at[:, span(p, h)]
        return pltpu.make_async_remote_copy(
            src_ref=ref, dst_ref=ref, send_sem=x_send.at[p], recv_sem=x_recv.at[p],
            device_id=(e, h_x), device_id_type=MESH)

    def c_copy(p, k):
        ref = output(p).at[:, span(p, (h, h_x)[k])]
        return pltpu.make_async_remote_copy(
            src_ref=ref, dst_ref=ref, send_sem=c_send.at[p, k], recv_sem=c_recv.at[p, k],
            device_id=(e, h_core), device_id_type=MESH)

    for p in range(PASSES):
        for d in (1, 2, 0):
            a_copy(p, d).start()
        buf[p, e, pl.ds(pl.multiple_of(h * rows, rows), rows), :] = source(p)[:, span(p, h)]

    @pl.loop(0, groups)
    def _(g):
        ids = picks_ref[...] - g * block
        lane = lax.broadcasted_iota(jnp.int32, (ids.shape[0], block), 1)
        hot[g] = jnp.where(ids == lane, 1.0, 0.0).astype(jnp.bfloat16)

    def own(p):
        for d in range(3):
            a_copy(p, d).wait_recv()

        @pl.when(z < nz - 1)
        def _():
            up(p, 1).start()

        @pl.when(z > 0)
        def _():
            dn(p, 1).start()

        across(p, 0, z).start()

    def step(p, s):
        @pl.when(z >= s)
        def _():
            up(p, s).wait_recv()
            if s < nz - 1:
                @pl.when(z < nz - 1)
                def _():
                    up(p, s + 1).start()
            across(p, s, z - s).start()

        @pl.when(z <= nz - 1 - s)
        def _():
            dn(p, s).wait_recv()
            if s < nz - 1:
                @pl.when(z > 0)
                def _():
                    dn(p, s + 1).start()
            across(p, nz - 1 + s, z + s).start()

    def gathered(p):
        across(p, 0, z).wait_recv()
        for s in range(1, nz):
            @pl.when(z >= s)
            def _():
                across(p, s, z - s).wait_recv()

            @pl.when(z <= nz - 1 - s)
            def _():
                across(p, nz - 1 + s, z + s).wait_recv()

    def pick(p):
        step_rows = 256
        out = output(p)

        @pl.loop(0, out.shape[0] // step_rows)
        def _(r):
            here = pl.ds(pl.multiple_of(r * step_rows, step_rows), step_rows)
            acc = jnp.zeros((step_rows, part), jnp.float32)
            for g in range(groups):
                acc += jnp.dot(hot[g, here, :], buf[p, g], preferred_element_type=jnp.float32)
            out[here, span(p, h)] = acc.astype(jnp.bfloat16)

        x_copy(p).start()
        c_copy(p, 0).start()

    def forward(p):
        x_copy(p).wait_recv()
        c_copy(p, 1).start()

    own(0)
    own(1)
    for p in range(PASSES):
        step(p, 1)
        if p + 2 < PASSES:
            own(p + 2)
        for s in range(2, nz):
            step(p, s)
        gathered(p)
        pick(p)
        if p > 0:
            forward(p - 1)
    forward(PASSES - 1)

    for p in range(PASSES):
        for d in range(3):
            a_copy(p, d).wait_send()

        @pl.when(z < nz - 1)
        def _():
            up(p, 1).wait_send()

        @pl.when(z > 0)
        def _():
            dn(p, 1).wait_send()

        across(p, 0, z).wait_send()
        for s in range(1, nz):
            @pl.when(z >= s)
            def _():
                if s < nz - 1:
                    @pl.when(z < nz - 1)
                    def _():
                        up(p, s + 1).wait_send()
                across(p, s, z - s).wait_send()

            @pl.when(z <= nz - 1 - s)
            def _():
                if s < nz - 1:
                    @pl.when(z > 0)
                    def _():
                        dn(p, s + 1).wait_send()
                across(p, nz - 1 + s, z + s).wait_send()

        x_copy(p).wait_send()
        for k in range(2):
            c_copy(p, k).wait()


def dispatch(tokens, grad_out, picks):
    groups = lax.axis_size("expert")
    nz = groups // 2
    rows, width = tokens.shape
    total = picks.size
    part = width // 4 // (PASSES // 2)
    dma = pltpu.SemaphoreType.DMA
    out = jax.ShapeDtypeStruct((total, width), jnp.bfloat16)
    return pl.pallas_call(
        functools.partial(dispatch_kernel, nz),
        out_shape=(out, out),
        in_specs=[pl.BlockSpec(memory_space=pltpu.VMEM)] * 3,
        out_specs=[pl.BlockSpec(memory_space=pltpu.VMEM)] * 2,
        scratch_shapes=[
            pltpu.VMEM((PASSES, groups, 4 * rows, part), jnp.bfloat16),
            pltpu.VMEM((groups, total, 4 * rows), jnp.bfloat16),
            dma((PASSES, 3)), dma((PASSES, 3)),
            dma((PASSES, nz - 1)), dma((PASSES, nz - 1)),
            dma((PASSES, nz - 1)), dma((PASSES, nz - 1)),
            dma((PASSES, 2 * nz - 1)), dma((PASSES, 2 * nz - 1)),
            dma((PASSES,)), dma((PASSES,)),
            dma((PASSES, 2)), dma((PASSES, 2)),
        ],
        compiler_params=pltpu.CompilerParams(
            collective_id=0, has_side_effects=True, vmem_limit_bytes=48 * 1024 * 1024),
        name="dispatch",
    )(tokens, grad_out, picks.reshape(total, 1))


def local(tokens, grad_out, picks, gates, w_gate, w_up, w_down):
    groups = lax.axis_size("expert")
    shares = lax.axis_size("hidden")
    tok_rows, width = tokens.shape
    exp_local, capacity = picks.shape
    total = groups * shares * tok_rows
    cols = width // shares
    flat = picks.reshape(-1)

    def spread(rows):
        part = lax.all_to_all(rows, "hidden", split_axis=1, concat_axis=0, tiled=True)
        return lax.all_gather(part, "expert", axis=0, tiled=True)

    def collect(everything):
        mine = everything[flat]
        return lax.all_gather(mine, "hidden", axis=1, tiled=True).reshape(exp_local, capacity, width)

    fits = shares == 4 and groups % 2 == 0 and total * cols <= 4 * 1024 * 1024
    if fits:
        picked, picked_grad = dispatch(tokens, grad_out, picks)
        picked = picked.reshape(exp_local, capacity, width)
        picked_grad = picked_grad.reshape(exp_local, capacity, width)
    else:
        picked_grad = collect(spread(grad_out))
        picked = collect(spread(tokens))
    back = jnp.einsum("xcd,xhd->xch", picked_grad, w_down, preferred_element_type=jnp.float32)
    gate = jnp.einsum("xcd,xhd->xch", picked, w_gate, preferred_element_type=jnp.float32)
    up = jnp.einsum("xcd,xhd->xch", picked, w_up, preferred_element_type=jnp.float32)
    sig = jax.nn.sigmoid(gate)
    act = gate * sig
    hid = (act * up).astype(jnp.bfloat16)
    score_part = jnp.sum(hid.astype(jnp.float32) * back, axis=-1)
    grad_scores = lax.psum(score_part, "hidden")
    grad_hid = gates[:, :, None] * back
    grad_gate = (grad_hid * up * sig * (1.0 + gate * (1.0 - sig))).astype(jnp.bfloat16)
    grad_up = (grad_hid * act).astype(jnp.bfloat16)
    weighted = (gates[:, :, None] * hid.astype(jnp.float32)).astype(jnp.bfloat16)
    partial_rows = (
        jnp.einsum("xch,xhd->xcd", grad_gate, w_gate, preferred_element_type=jnp.float32)
        + jnp.einsum("xch,xhd->xcd", grad_up, w_up, preferred_element_type=jnp.float32)
    ).astype(jnp.bfloat16)
    rows_grad = lax.psum_scatter(
        partial_rows.reshape(exp_local * capacity, width), "hidden", scatter_dimension=1, tiled=True
    )
    selector = (jnp.arange(total, dtype=jnp.int32)[:, None] == flat[None, :]).astype(jnp.bfloat16)
    sums = jnp.dot(selector, rows_grad, preferred_element_type=jnp.float32).astype(jnp.bfloat16)
    own = lax.psum_scatter(sums, "expert", scatter_dimension=0, tiled=True)
    grad_tokens = lax.all_to_all(own, "hidden", split_axis=0, concat_axis=1, tiled=True)
    grad_w_down = jnp.einsum(
        "xch,xcd->xhd", weighted, picked_grad, preferred_element_type=jnp.float32
    ).astype(jnp.bfloat16)
    grad_w_gate = jnp.einsum(
        "xch,xcd->xhd", grad_gate, picked, preferred_element_type=jnp.float32
    ).astype(jnp.bfloat16)
    grad_w_up = jnp.einsum(
        "xch,xcd->xhd", grad_up, picked, preferred_element_type=jnp.float32
    ).astype(jnp.bfloat16)
    return (grad_tokens, grad_scores, grad_w_gate, grad_w_up, grad_w_down)


def solution(mesh):
    placed = (
        P(("expert", "hidden"), None),
        P(("expert", "hidden"), None),
        P("expert", None),
        P("expert", None),
        P("expert", "hidden", None),
        P("expert", "hidden", None),
        P("expert", "hidden", None),
    )
    return jax.shard_map(
        local,
        mesh=mesh,
        in_specs=placed,
        out_specs=(
            P(("expert", "hidden"), None),
            P("expert", None),
            P("expert", "hidden", None),
            P("expert", "hidden", None),
            P("expert", "hidden", None),
        ),
        check_vma=False,
    )
```

```python
import functools
import jax
import jax.numpy as jnp
from jax import lax
from jax.experimental import pallas as pl
from jax.experimental.pallas import tpu as pltpu
from jax.sharding import PartitionSpec as P

MESH = pl.DeviceIdType.MESH
PASSES = 4


def dispatch_kernel(
    nz, tok_ref, grad_ref, picks_ref, out_tok, out_grad, buf, hot,
    a_send, a_recv, up_send, up_recv, dn_send, dn_recv, y_send, y_recv,
    x_send, x_recv, c_send, c_recv,
):
    e, h = lax.axis_index("expert"), lax.axis_index("hidden")
    z, y = e // 2, e % 2
    h_core = h + 1 - 2 * (h % 2)
    h_x = (h + 2) % 4
    h_far = (h_core + 2) % 4
    rows, width = tok_ref.shape
    cols = width // 4
    part = buf.shape[-1]
    halves = cols // part
    peers = (h_core, h_x, h_far)
    groups = 2 * nz
    block = 4 * rows

    barrier = pltpu.get_barrier_semaphore()
    for peer in peers:
        pl.semaphore_signal(barrier, inc=1, device_id=(e, peer), device_id_type=MESH)
    pl.semaphore_signal(barrier, inc=1, device_id=(z * 2 + 1 - y, h), device_id_type=MESH)

    @pl.when(z > 0)
    def _():
        pl.semaphore_signal(barrier, inc=1, device_id=(e - 2, h), device_id_type=MESH)

    @pl.when(z < nz - 1)
    def _():
        pl.semaphore_signal(barrier, inc=1, device_id=(e + 2, h), device_id_type=MESH)

    ends = jnp.where(z == 0, 1, 0) + jnp.where(z == nz - 1, 1, 0)
    pl.semaphore_wait(barrier, 6 - ends)

    def source(p):
        return (tok_ref, grad_ref)[p // halves]

    def output(p):
        return (out_tok, out_grad)[p // halves]

    def span(p, owner):
        return pl.ds(pl.multiple_of(owner * cols + (p % halves) * part, part), part)

    def mine(p):
        return buf.at[p, e, pl.ds(pl.multiple_of(h * rows, rows), rows), :]

    def a_copy(p, d):
        return pltpu.make_async_remote_copy(
            src_ref=source(p).at[:, span(p, peers[d])], dst_ref=mine(p),
            send_sem=a_send.at[p, d], recv_sem=a_recv.at[p, d],
            device_id=(e, peers[d]), device_id_type=MESH)

    def chunk_copy(p, zz, send, recv, target):
        ref = buf.at[p, zz * 2 + y]
        return pltpu.make_async_remote_copy(
            src_ref=ref, dst_ref=ref, send_sem=send, recv_sem=recv,
            device_id=(target, h), device_id_type=MESH)

    def up(p, s):
        return chunk_copy(p, z - (s - 1), up_send.at[p, s - 1], up_recv.at[p, s - 1], e + 2)

    def dn(p, s):
        return chunk_copy(p, z + (s - 1), dn_send.at[p, s - 1], dn_recv.at[p, s - 1], e - 2)

    def across(p, k, zz):
        return chunk_copy(p, zz, y_send.at[p, k], y_recv.at[p, k], z * 2 + 1 - y)

    def x_copy(p):
        ref = output(p).at[:, span(p, h)]
        return pltpu.make_async_remote_copy(
            src_ref=ref, dst_ref=ref, send_sem=x_send.at[p], recv_sem=x_recv.at[p],
            device_id=(e, h_x), device_id_type=MESH)

    def c_copy(p, k):
        ref = output(p).at[:, span(p, (h, h_x)[k])]
        return pltpu.make_async_remote_copy(
            src_ref=ref, dst_ref=ref, send_sem=c_send.at[p, k], recv_sem=c_recv.at[p, k],
            device_id=(e, h_core), device_id_type=MESH)

    for p in range(PASSES):
        for d in (1, 2, 0):
            a_copy(p, d).start()
        buf[p, e, pl.ds(pl.multiple_of(h * rows, rows), rows), :] = source(p)[:, span(p, h)]

    @pl.loop(0, groups)
    def _(g):
        ids = picks_ref[...] - g * block
        lane = lax.broadcasted_iota(jnp.int32, (ids.shape[0], block), 1)
        hot[g] = jnp.where(ids == lane, 1.0, 0.0).astype(jnp.bfloat16)

    def own(p):
        for d in range(3):
            a_copy(p, d).wait_recv()

        @pl.when(z < nz - 1)
        def _():
            up(p, 1).start()

        @pl.when(z > 0)
        def _():
            dn(p, 1).start()

        across(p, 0, z).start()

    def step(p, s):
        @pl.when(z >= s)
        def _():
            up(p, s).wait_recv()
            if s < nz - 1:
                @pl.when(z < nz - 1)
                def _():
                    up(p, s + 1).start()
            across(p, s, z - s).start()

        @pl.when(z <= nz - 1 - s)
        def _():
            dn(p, s).wait_recv()
            if s < nz - 1:
                @pl.when(z > 0)
                def _():
                    dn(p, s + 1).start()
            across(p, nz - 1 + s, z + s).start()

    def gathered(p):
        across(p, 0, z).wait_recv()
        for s in range(1, nz):
            @pl.when(z >= s)
            def _():
                across(p, s, z - s).wait_recv()

            @pl.when(z <= nz - 1 - s)
            def _():
                across(p, nz - 1 + s, z + s).wait_recv()

    def pick(p):
        step_rows = 256
        out = output(p)

        @pl.loop(0, out.shape[0] // step_rows)
        def _(r):
            here = pl.ds(pl.multiple_of(r * step_rows, step_rows), step_rows)
            acc = jnp.zeros((step_rows, part), jnp.float32)
            for g in range(groups):
                acc += jnp.dot(hot[g, here, :], buf[p, g], preferred_element_type=jnp.float32)
            out[here, span(p, h)] = acc.astype(jnp.bfloat16)

        x_copy(p).start()
        c_copy(p, 0).start()

    def forward(p):
        x_copy(p).wait_recv()
        c_copy(p, 1).start()

    own(0)
    own(1)
    for p in range(PASSES):
        step(p, 1)
        if p + 2 < PASSES:
            own(p + 2)
        for s in range(2, nz):
            step(p, s)
        gathered(p)
        pick(p)
        if p > 0:
            forward(p - 1)
    forward(PASSES - 1)

    for p in range(PASSES):
        for d in range(3):
            a_copy(p, d).wait_send()

        @pl.when(z < nz - 1)
        def _():
            up(p, 1).wait_send()

        @pl.when(z > 0)
        def _():
            dn(p, 1).wait_send()

        across(p, 0, z).wait_send()
        for s in range(1, nz):
            @pl.when(z >= s)
            def _():
                if s < nz - 1:
                    @pl.when(z < nz - 1)
                    def _():
                        up(p, s + 1).wait_send()
                across(p, s, z - s).wait_send()

            @pl.when(z <= nz - 1 - s)
            def _():
                if s < nz - 1:
                    @pl.when(z > 0)
                    def _():
                        dn(p, s + 1).wait_send()
                across(p, nz - 1 + s, z + s).wait_send()

        x_copy(p).wait_send()
        for k in range(2):
            c_copy(p, k).wait()


def dispatch(tokens, grad_out, picks):
    groups = lax.axis_size("expert")
    nz = groups // 2
    rows, width = tokens.shape
    total = picks.size
    part = width // 4 // (PASSES // 2)
    dma = pltpu.SemaphoreType.DMA
    out = jax.ShapeDtypeStruct((total, width), jnp.bfloat16)
    return pl.pallas_call(
        functools.partial(dispatch_kernel, nz),
        out_shape=(out, out),
        in_specs=[pl.BlockSpec(memory_space=pltpu.VMEM)] * 3,
        out_specs=[pl.BlockSpec(memory_space=pltpu.VMEM)] * 2,
        scratch_shapes=[
            pltpu.VMEM((PASSES, groups, 4 * rows, part), jnp.bfloat16),
            pltpu.VMEM((groups, total, 4 * rows), jnp.bfloat16),
            dma((PASSES, 3)), dma((PASSES, 3)),
            dma((PASSES, nz - 1)), dma((PASSES, nz - 1)),
            dma((PASSES, nz - 1)), dma((PASSES, nz - 1)),
            dma((PASSES, 2 * nz - 1)), dma((PASSES, 2 * nz - 1)),
            dma((PASSES,)), dma((PASSES,)),
            dma((PASSES, 2)), dma((PASSES, 2)),
        ],
        compiler_params=pltpu.CompilerParams(
            collective_id=0, has_side_effects=True, vmem_limit_bytes=48 * 1024 * 1024),
        name="dispatch",
    )(tokens, grad_out, picks.reshape(total, 1))


BACK = 4


def combine_kernel(
    nz, part_ref, ids_ref, score_ref, out, score_out, near, x_out, x_in, hot, y_out, y_in, keep,
    dn_out, dn_in, up_out, up_in, fin, scores,
    a_send, a_recv, x_send, x_recv, y_send, y_recv, dn_send, dn_recv, up_send, up_recv,
    f_send, f_recv, s_send, s_recv,
):
    e, h = lax.axis_index("expert"), lax.axis_index("hidden")
    z, y = e // 2, e % 2
    h_core = h + 1 - 2 * (h % 2)
    h_x = (h + 2) % 4
    h_far = (h_core + 2) % 4
    peers = (h_core, h_x, h_far)
    count, width = part_ref.shape
    cols = width // 4
    wide = cols // BACK
    groups = 2 * nz
    rows = out.shape[0]
    block = 4 * rows

    barrier = pltpu.get_barrier_semaphore()
    for peer in peers:
        pl.semaphore_signal(barrier, inc=1, device_id=(e, peer), device_id_type=MESH)
    pl.semaphore_signal(barrier, inc=1, device_id=(z * 2 + 1 - y, h), device_id_type=MESH)

    @pl.when(z > 0)
    def _():
        pl.semaphore_signal(barrier, inc=1, device_id=(e - 2, h), device_id_type=MESH)

    @pl.when(z < nz - 1)
    def _():
        pl.semaphore_signal(barrier, inc=1, device_id=(e + 2, h), device_id_type=MESH)

    ends = jnp.where(z == 0, 1, 0) + jnp.where(z == nz - 1, 1, 0)
    pl.semaphore_wait(barrier, 6 - ends)

    def span(q, owner):
        return pl.ds(pl.multiple_of(owner * cols + q * wide, wide), wide)

    def remote(src, dst, send, recv, target):
        return pltpu.make_async_remote_copy(
            src_ref=src, dst_ref=dst, send_sem=send, recv_sem=recv,
            device_id=target, device_id_type=MESH)

    def a_copy(q, k):
        return remote(part_ref.at[:, span(q, (h_core, h_far)[k])], near.at[q, k],
                      a_send.at[q, k], a_recv.at[q, k], (e, h_core))

    def x_copy(q):
        return remote(x_out.at[q], x_in.at[q], x_send.at[q], x_recv.at[q], (e, h_x))

    def y_copy(q, zz):
        return remote(y_out.at[q, zz], y_in.at[q, zz], y_send.at[q, zz], y_recv.at[q, zz],
                      (z * 2 + 1 - y, h))

    def dn_copy(q, j):
        return remote(dn_out.at[q, j - 1], dn_in.at[q, j - 1], dn_send.at[q, j - 1],
                      dn_recv.at[q, j - 1], (e - 2, h))

    def up_copy(q, j):
        return remote(up_out.at[q, j - 1], up_in.at[q, j - 1], up_send.at[q, j - 1],
                      up_recv.at[q, j - 1], (e + 2, h))

    def f_copy(q, d):
        return remote(fin.at[q, pl.ds(pl.multiple_of(peers[d] * rows, rows), rows), :],
                      out.at[:, span(q, h)], f_send.at[q, d], f_recv.at[q, d], (e, peers[d]))

    def s_copy(d):
        return remote(score_ref, scores.at[h], s_send.at[d], s_recv.at[d], (e, peers[d]))

    for q in range(BACK):
        a_copy(q, 1).start()
        a_copy(q, 0).start()
    for d in range(3):
        s_copy(d).start()
    scores[h] = score_ref[...]

    def hidden_send(q):
        a_copy(q, 1).wait_recv()
        both = part_ref[:, span(q, h_x)].astype(jnp.float32) + near[q, 1].astype(jnp.float32)
        x_out[q] = both.astype(jnp.bfloat16)
        x_copy(q).start()

    def spread_rows(q):
        a_copy(q, 0).wait_recv()
        both = part_ref[:, span(q, h)].astype(jnp.float32) + near[q, 0].astype(jnp.float32)
        x_copy(q).wait_recv()
        near[q, 0] = (both + x_in[q].astype(jnp.float32)).astype(jnp.bfloat16)
        for zz in range(nz):
            y_out[q, zz] = jnp.dot(
                hot[zz * 2 + 1 - y], near[q, 0], preferred_element_type=jnp.float32
            ).astype(jnp.bfloat16)
            y_copy(q, zz).start()
        for zz in range(nz):
            keep[q, zz] = jnp.dot(hot[zz * 2 + y], near[q, 0], preferred_element_type=jnp.float32)

    def line(q, j):
        @pl.when(z >= j)
        def _():
            @pl.when(z < nz - 1)
            def _():
                if j < nz - 1:
                    dn_copy(q, j + 1).wait_recv()
                    keep[q, z - j] += dn_in[q, j].astype(jnp.float32)
            dn_out[q, j - 1] = keep[q, z - j].astype(jnp.bfloat16)
            dn_copy(q, j).start()

        @pl.when(z <= nz - 1 - j)
        def _():
            @pl.when(z > 0)
            def _():
                if j < nz - 1:
                    up_copy(q, j + 1).wait_recv()
                    keep[q, z + j] += up_in[q, j].astype(jnp.float32)
            up_out[q, j - 1] = keep[q, z + j].astype(jnp.bfloat16)
            up_copy(q, j).start()

    def far(q):
        for zz in range(nz):
            y_copy(q, zz).wait_recv()
            keep[q, zz] += y_in[q, zz].astype(jnp.float32)
        for j in range(nz - 1, 1, -1):
            line(q, j)

    def close(q):
        line(q, 1)

        @pl.when(z < nz - 1)
        def _():
            dn_copy(q, 1).wait_recv()
            keep[q, z] += dn_in[q, 0].astype(jnp.float32)

        @pl.when(z > 0)
        def _():
            up_copy(q, 1).wait_recv()
            keep[q, z] += up_in[q, 0].astype(jnp.float32)

        fin[q] = keep[q, z].astype(jnp.bfloat16)
        for d in range(3):
            f_copy(q, d).start()
        out[:, span(q, h)] = fin[q, pl.ds(pl.multiple_of(h * rows, rows), rows), :]

    hidden_send(0)
    hidden_send(1)

    @pl.loop(0, groups)
    def _(g):
        ids = ids_ref[...] - g * block
        row = lax.broadcasted_iota(jnp.int32, (block, count), 0)
        hot[g] = jnp.where(ids == row, 1.0, 0.0).astype(jnp.bfloat16)

    hidden_send(2)
    hidden_send(3)
    spread_rows(0)
    spread_rows(1)
    far(0)
    spread_rows(2)
    close(0)
    far(1)
    spread_rows(3)
    close(1)
    far(2)
    close(2)
    far(3)
    close(3)

    for d in range(3):
        s_copy(d).wait()
    score_out[...] = scores[0] + scores[1] + scores[2] + scores[3]

    for q in range(BACK):
        for k in range(2):
            a_copy(q, k).wait_send()
        x_copy(q).wait_send()
        for zz in range(nz):
            y_copy(q, zz).wait_send()
        for j in range(1, nz):
            @pl.when(z >= j)
            def _():
                dn_copy(q, j).wait_send()

            @pl.when(z <= nz - 1 - j)
            def _():
                up_copy(q, j).wait_send()
        for d in range(3):
            f_copy(q, d).wait()


def combine(partial_rows, picks, score_part, rows):
    groups = lax.axis_size("expert")
    nz = groups // 2
    count, width = partial_rows.shape
    wide = width // 4 // BACK
    block = 4 * rows
    dma = pltpu.SemaphoreType.DMA
    low = jnp.bfloat16
    vmem = pl.BlockSpec(memory_space=pltpu.VMEM)
    line = pltpu.VMEM((BACK, nz - 1, block, wide), low)
    out, scores = pl.pallas_call(
        functools.partial(combine_kernel, nz),
        out_shape=(
            jax.ShapeDtypeStruct((rows, width), low),
            jax.ShapeDtypeStruct((count // 128, 128), jnp.float32),
        ),
        in_specs=[vmem] * 3,
        out_specs=[vmem] * 2,
        scratch_shapes=[
            pltpu.VMEM((BACK, 2, count, wide), low),
            pltpu.VMEM((BACK, count, wide), low),
            pltpu.VMEM((BACK, count, wide), low),
            pltpu.VMEM((groups, block, count), low),
            pltpu.VMEM((BACK, nz, block, wide), low),
            pltpu.VMEM((BACK, nz, block, wide), low),
            pltpu.VMEM((BACK, nz, block, wide), jnp.float32),
            line, line, line, line,
            pltpu.VMEM((BACK, block, wide), low),
            pltpu.VMEM((4, count // 128, 128), jnp.float32),
            dma((BACK, 2)), dma((BACK, 2)), dma((BACK,)), dma((BACK,)),
            dma((BACK, nz)), dma((BACK, nz)),
            dma((BACK, nz - 1)), dma((BACK, nz - 1)), dma((BACK, nz - 1)), dma((BACK, nz - 1)),
            dma((BACK, 3)), dma((BACK, 3)), dma((3,)), dma((3,)),
        ],
        compiler_params=pltpu.CompilerParams(
            collective_id=1, has_side_effects=True, vmem_limit_bytes=48 * 1024 * 1024),
        name="combine",
    )(partial_rows, picks.reshape(1, count), score_part.reshape(count // 128, 128))
    return out, scores.reshape(score_part.shape)


def local(tokens, grad_out, picks, gates, w_gate, w_up, w_down):
    groups = lax.axis_size("expert")
    shares = lax.axis_size("hidden")
    tok_rows, width = tokens.shape
    exp_local, capacity = picks.shape
    total = groups * shares * tok_rows
    cols = width // shares
    flat = picks.reshape(-1)

    def spread(rows):
        part = lax.all_to_all(rows, "hidden", split_axis=1, concat_axis=0, tiled=True)
        return lax.all_gather(part, "expert", axis=0, tiled=True)

    def collect(everything):
        mine = everything[flat]
        return lax.all_gather(mine, "hidden", axis=1, tiled=True).reshape(exp_local, capacity, width)

    fits = shares == 4 and groups % 2 == 0 and total * cols <= 4 * 1024 * 1024
    if fits:
        picked, picked_grad = dispatch(tokens, grad_out, picks)
        picked = picked.reshape(exp_local, capacity, width)
        picked_grad = picked_grad.reshape(exp_local, capacity, width)
    else:
        picked_grad = collect(spread(grad_out))
        picked = collect(spread(tokens))
    back = jnp.einsum("xcd,xhd->xch", picked_grad, w_down, preferred_element_type=jnp.float32)
    gate = jnp.einsum("xcd,xhd->xch", picked, w_gate, preferred_element_type=jnp.float32)
    up = jnp.einsum("xcd,xhd->xch", picked, w_up, preferred_element_type=jnp.float32)
    sig = jax.nn.sigmoid(gate)
    act = gate * sig
    hid = (act * up).astype(jnp.bfloat16)
    score_part = jnp.sum(hid.astype(jnp.float32) * back, axis=-1)
    grad_hid = gates[:, :, None] * back
    grad_gate = (grad_hid * up * sig * (1.0 + gate * (1.0 - sig))).astype(jnp.bfloat16)
    grad_up = (grad_hid * act).astype(jnp.bfloat16)
    weighted = (gates[:, :, None] * hid.astype(jnp.float32)).astype(jnp.bfloat16)
    partial_rows = (
        jnp.einsum("xch,xhd->xcd", grad_gate, w_gate, preferred_element_type=jnp.float32)
        + jnp.einsum("xch,xhd->xcd", grad_up, w_up, preferred_element_type=jnp.float32)
    ).astype(jnp.bfloat16)
    if fits:
        grad_tokens, grad_scores = combine(
            partial_rows.reshape(exp_local * capacity, width), picks, score_part, tok_rows
        )
    else:
        grad_scores = lax.psum(score_part, "hidden")
        rows_grad = lax.psum_scatter(
            partial_rows.reshape(exp_local * capacity, width), "hidden", scatter_dimension=1, tiled=True
        )
        selector = (jnp.arange(total, dtype=jnp.int32)[:, None] == flat[None, :]).astype(jnp.bfloat16)
        sums = jnp.dot(selector, rows_grad, preferred_element_type=jnp.float32).astype(jnp.bfloat16)
        own = lax.psum_scatter(sums, "expert", scatter_dimension=0, tiled=True)
        grad_tokens = lax.all_to_all(own, "hidden", split_axis=0, concat_axis=1, tiled=True)
    grad_w_down = jnp.einsum(
        "xch,xcd->xhd", weighted, picked_grad, preferred_element_type=jnp.float32
    ).astype(jnp.bfloat16)
    grad_w_gate = jnp.einsum(
        "xch,xcd->xhd", grad_gate, picked, preferred_element_type=jnp.float32
    ).astype(jnp.bfloat16)
    grad_w_up = jnp.einsum(
        "xch,xcd->xhd", grad_up, picked, preferred_element_type=jnp.float32
    ).astype(jnp.bfloat16)
    return (grad_tokens, grad_scores, grad_w_gate, grad_w_up, grad_w_down)


def solution(mesh):
    placed = (
        P(("expert", "hidden"), None),
        P(("expert", "hidden"), None),
        P("expert", None),
        P("expert", None),
        P("expert", "hidden", None),
        P("expert", "hidden", None),
        P("expert", "hidden", None),
    )
    return jax.shard_map(
        local,
        mesh=mesh,
        in_specs=placed,
        out_specs=(
            P(("expert", "hidden"), None),
            P("expert", None),
            P("expert", "hidden", None),
            P("expert", "hidden", None),
            P("expert", "hidden", None),
        ),
        check_vma=False,
    )
```

```python
import functools
import jax
import jax.numpy as jnp
from jax import lax
from jax.experimental import pallas as pl
from jax.experimental.pallas import tpu as pltpu
from jax.sharding import PartitionSpec as P

MESH = pl.DeviceIdType.MESH
PASSES = 4


def dispatch_kernel(
    nz, tok_ref, grad_ref, picks_ref, out_tok, out_grad, buf, hot,
    a_send, a_recv, up_send, up_recv, dn_send, dn_recv, y_send, y_recv,
    x_send, x_recv, c_send, c_recv, e_send, e_recv,
):
    e, h = lax.axis_index("expert"), lax.axis_index("hidden")
    z, y = e // 2, e % 2
    h_core = h + 1 - 2 * (h % 2)
    h_x = (h + 2) % 4
    h_far = (h_core + 2) % 4
    rows, width = tok_ref.shape
    cols = width // 4
    part = buf.shape[-1]
    halves = cols // part
    peers = (h_core, h_x, h_far)
    groups = 2 * nz
    block = 4 * rows

    barrier = pltpu.get_barrier_semaphore()
    for peer in peers:
        pl.semaphore_signal(barrier, inc=1, device_id=(e, peer), device_id_type=MESH)
    pl.semaphore_signal(barrier, inc=1, device_id=(z * 2 + 1 - y, h), device_id_type=MESH)

    @pl.when(z > 0)
    def _():
        pl.semaphore_signal(barrier, inc=1, device_id=(e - 2, h), device_id_type=MESH)

    @pl.when(z < nz - 1)
    def _():
        pl.semaphore_signal(barrier, inc=1, device_id=(e + 2, h), device_id_type=MESH)

    ends = jnp.where(z == 0, 1, 0) + jnp.where(z == nz - 1, 1, 0)
    pl.semaphore_wait(barrier, 6 - ends)

    def source(p):
        return (tok_ref, grad_ref)[p // halves]

    def output(p):
        return (out_tok, out_grad)[p // halves]

    def span(p, owner):
        return pl.ds(pl.multiple_of(owner * cols + (p % halves) * part, part), part)

    def mine(p):
        return buf.at[p, e, pl.ds(pl.multiple_of(h * rows, rows), rows), :]

    def a_copy(p, d):
        return pltpu.make_async_remote_copy(
            src_ref=source(p).at[:, span(p, peers[d])], dst_ref=mine(p),
            send_sem=a_send.at[p, d], recv_sem=a_recv.at[p, d],
            device_id=(e, peers[d]), device_id_type=MESH)

    def chunk_copy(p, zz, send, recv, target):
        ref = buf.at[p, zz * 2 + y]
        return pltpu.make_async_remote_copy(
            src_ref=ref, dst_ref=ref, send_sem=send, recv_sem=recv,
            device_id=(target, h), device_id_type=MESH)

    def up(p, s):
        return chunk_copy(p, z - (s - 1), up_send.at[p, s - 1], up_recv.at[p, s - 1], e + 2)

    def dn(p, s):
        return chunk_copy(p, z + (s - 1), dn_send.at[p, s - 1], dn_recv.at[p, s - 1], e - 2)

    def across(p, k, zz):
        return chunk_copy(p, zz, y_send.at[p, k], y_recv.at[p, k], z * 2 + 1 - y)

    def part_copy(p, group, first, send, recv, target):
        ref = buf.at[p, group, pl.ds(first, block // 2), :]
        return pltpu.make_async_remote_copy(
            src_ref=ref, dst_ref=ref, send_sem=send, recv_sem=recv,
            device_id=(target, h), device_id_type=MESH)

    def across_half(p, k, zz):
        return part_copy(p, zz * 2 + y, 0, y_send.at[p, k], y_recv.at[p, k], z * 2 + 1 - y)

    def extra(p, zz, target):
        return part_copy(p, zz * 2 + 1 - y, block // 2, e_send.at[p], e_recv.at[p], target)

    def across_do(p, s, act):
        at_top, at_low = z == nz - 1, z == 0

        @pl.when(z >= s)
        def _():
            if s > 1:
                act(across(p, s, z - s))
            else:
                @pl.when(at_top)
                def _():
                    act(across_half(p, s, z - s))

                @pl.when(z < nz - 1)
                def _():
                    act(across(p, s, z - s))

        @pl.when(z <= nz - 1 - s)
        def _():
            if s > 1:
                act(across(p, nz - 1 + s, z + s))
            else:
                @pl.when(at_low)
                def _():
                    act(across_half(p, nz - 1 + s, z + s))

                @pl.when(z > 0)
                def _():
                    act(across(p, nz - 1 + s, z + s))

    def relay(p):
        across(p, 0, z).wait_recv()

        @pl.when(z == 1)
        def _():
            extra(p, z, e - 2).start()

        @pl.when(z == nz - 2)
        def _():
            extra(p, z, e + 2).start()

    def x_copy(p):
        ref = output(p).at[:, span(p, h)]
        return pltpu.make_async_remote_copy(
            src_ref=ref, dst_ref=ref, send_sem=x_send.at[p], recv_sem=x_recv.at[p],
            device_id=(e, h_x), device_id_type=MESH)

    def c_copy(p, k):
        ref = output(p).at[:, span(p, (h, h_x)[k])]
        return pltpu.make_async_remote_copy(
            src_ref=ref, dst_ref=ref, send_sem=c_send.at[p, k], recv_sem=c_recv.at[p, k],
            device_id=(e, h_core), device_id_type=MESH)

    for p in range(PASSES):
        for d in (1, 2, 0):
            a_copy(p, d).start()
        buf[p, e, pl.ds(pl.multiple_of(h * rows, rows), rows), :] = source(p)[:, span(p, h)]

    @pl.loop(0, groups)
    def _(g):
        ids = picks_ref[...] - g * block
        lane = lax.broadcasted_iota(jnp.int32, (ids.shape[0], block), 1)
        hot[g] = jnp.where(ids == lane, 1.0, 0.0).astype(jnp.bfloat16)

    def own(p):
        for d in range(3):
            a_copy(p, d).wait_recv()

        @pl.when(z < nz - 1)
        def _():
            up(p, 1).start()

        @pl.when(z > 0)
        def _():
            dn(p, 1).start()

        across(p, 0, z).start()

    def step(p, s):
        @pl.when(z >= s)
        def _():
            up(p, s).wait_recv()
            if s < nz - 1:
                @pl.when(z < nz - 1)
                def _():
                    up(p, s + 1).start()

        @pl.when(z <= nz - 1 - s)
        def _():
            dn(p, s).wait_recv()
            if s < nz - 1:
                @pl.when(z > 0)
                def _():
                    dn(p, s + 1).start()

        across_do(p, s, lambda copy: copy.start())

    def gathered(p):
        for s in range(1, nz):
            across_do(p, s, lambda copy: copy.wait_recv())

        @pl.when(z == 0)
        def _():
            extra(p, 1, e).wait_recv()

        @pl.when(z == nz - 1)
        def _():
            extra(p, nz - 2, e).wait_recv()

    def pick(p):
        step_rows = 256
        out = output(p)

        @pl.loop(0, out.shape[0] // step_rows)
        def _(r):
            here = pl.ds(pl.multiple_of(r * step_rows, step_rows), step_rows)
            acc = jnp.zeros((step_rows, part), jnp.float32)
            for g in range(groups):
                acc += jnp.dot(hot[g, here, :], buf[p, g], preferred_element_type=jnp.float32)
            out[here, span(p, h)] = acc.astype(jnp.bfloat16)

        x_copy(p).start()
        c_copy(p, 0).start()

    def forward(p):
        x_copy(p).wait_recv()
        c_copy(p, 1).start()

    own(0)
    own(1)
    for p in range(PASSES):
        step(p, 1)
        if p + 2 < PASSES:
            own(p + 2)
        relay(p)
        for s in range(2, nz):
            step(p, s)
        gathered(p)
        pick(p)
        if p > 0:
            forward(p - 1)
    forward(PASSES - 1)

    for p in range(PASSES):
        for d in range(3):
            a_copy(p, d).wait_send()

        @pl.when(z < nz - 1)
        def _():
            up(p, 1).wait_send()

        @pl.when(z > 0)
        def _():
            dn(p, 1).wait_send()

        across(p, 0, z).wait_send()
        for s in range(1, nz):
            @pl.when(z >= s)
            def _():
                if s < nz - 1:
                    @pl.when(z < nz - 1)
                    def _():
                        up(p, s + 1).wait_send()

            @pl.when(z <= nz - 1 - s)
            def _():
                if s < nz - 1:
                    @pl.when(z > 0)
                    def _():
                        dn(p, s + 1).wait_send()
            across_do(p, s, lambda copy: copy.wait_send())

        @pl.when((z == 1) | (z == nz - 2))
        def _():
            extra(p, z, e).wait_send()

        x_copy(p).wait_send()
        for k in range(2):
            c_copy(p, k).wait()


def dispatch(tokens, grad_out, picks):
    groups = lax.axis_size("expert")
    nz = groups // 2
    rows, width = tokens.shape
    total = picks.size
    part = width // 4 // (PASSES // 2)
    dma = pltpu.SemaphoreType.DMA
    out = jax.ShapeDtypeStruct((total, width), jnp.bfloat16)
    return pl.pallas_call(
        functools.partial(dispatch_kernel, nz),
        out_shape=(out, out),
        in_specs=[pl.BlockSpec(memory_space=pltpu.VMEM)] * 3,
        out_specs=[pl.BlockSpec(memory_space=pltpu.VMEM)] * 2,
        scratch_shapes=[
            pltpu.VMEM((PASSES, groups, 4 * rows, part), jnp.bfloat16),
            pltpu.VMEM((groups, total, 4 * rows), jnp.bfloat16),
            dma((PASSES, 3)), dma((PASSES, 3)),
            dma((PASSES, nz - 1)), dma((PASSES, nz - 1)),
            dma((PASSES, nz - 1)), dma((PASSES, nz - 1)),
            dma((PASSES, 2 * nz - 1)), dma((PASSES, 2 * nz - 1)),
            dma((PASSES,)), dma((PASSES,)),
            dma((PASSES, 2)), dma((PASSES, 2)),
            dma((PASSES,)), dma((PASSES,)),
        ],
        compiler_params=pltpu.CompilerParams(
            collective_id=0, has_side_effects=True, vmem_limit_bytes=48 * 1024 * 1024),
        name="dispatch",
    )(tokens, grad_out, picks.reshape(total, 1))


BACK = 4


def combine_kernel(
    nz, part_ref, ids_ref, score_ref, out, score_out, near, x_out, x_in, hot, y_out, y_in, keep,
    dn_out, dn_in, up_out, up_in, fin, scores,
    a_send, a_recv, x_send, x_recv, y_send, y_recv, dn_send, dn_recv, up_send, up_recv,
    f_send, f_recv, s_send, s_recv,
):
    e, h = lax.axis_index("expert"), lax.axis_index("hidden")
    z, y = e // 2, e % 2
    h_core = h + 1 - 2 * (h % 2)
    h_x = (h + 2) % 4
    h_far = (h_core + 2) % 4
    peers = (h_core, h_x, h_far)
    count, width = part_ref.shape
    cols = width // 4
    wide = cols // BACK
    groups = 2 * nz
    rows = out.shape[0]
    block = 4 * rows

    barrier = pltpu.get_barrier_semaphore()
    for peer in peers:
        pl.semaphore_signal(barrier, inc=1, device_id=(e, peer), device_id_type=MESH)
    pl.semaphore_signal(barrier, inc=1, device_id=(z * 2 + 1 - y, h), device_id_type=MESH)

    @pl.when(z > 0)
    def _():
        pl.semaphore_signal(barrier, inc=1, device_id=(e - 2, h), device_id_type=MESH)

    @pl.when(z < nz - 1)
    def _():
        pl.semaphore_signal(barrier, inc=1, device_id=(e + 2, h), device_id_type=MESH)

    ends = jnp.where(z == 0, 1, 0) + jnp.where(z == nz - 1, 1, 0)
    pl.semaphore_wait(barrier, 6 - ends)

    def span(q, owner):
        return pl.ds(pl.multiple_of(owner * cols + q * wide, wide), wide)

    def remote(src, dst, send, recv, target):
        return pltpu.make_async_remote_copy(
            src_ref=src, dst_ref=dst, send_sem=send, recv_sem=recv,
            device_id=target, device_id_type=MESH)

    def a_copy(q, k):
        return remote(part_ref.at[:, span(q, (h_core, h_far)[k])], near.at[q, k],
                      a_send.at[q, k], a_recv.at[q, k], (e, h_core))

    def x_copy(q):
        return remote(x_out.at[q], x_in.at[q], x_send.at[q], x_recv.at[q], (e, h_x))

    def y_copy(q, zz):
        return remote(y_out.at[q, zz], y_in.at[q, zz], y_send.at[q, zz], y_recv.at[q, zz],
                      (z * 2 + 1 - y, h))

    def dn_copy(q, j):
        return remote(dn_out.at[q, j - 1], dn_in.at[q, j - 1], dn_send.at[q, j - 1],
                      dn_recv.at[q, j - 1], (e - 2, h))

    def up_copy(q, j):
        return remote(up_out.at[q, j - 1], up_in.at[q, j - 1], up_send.at[q, j - 1],
                      up_recv.at[q, j - 1], (e + 2, h))

    def f_copy(q, d):
        return remote(fin.at[q, pl.ds(pl.multiple_of(peers[d] * rows, rows), rows), :],
                      out.at[:, span(q, h)], f_send.at[q, d], f_recv.at[q, d], (e, peers[d]))

    def s_copy(d):
        return remote(score_ref, scores.at[h], s_send.at[d], s_recv.at[d], (e, peers[d]))

    for q in range(BACK):
        a_copy(q, 1).start()
        a_copy(q, 0).start()
    for d in range(3):
        s_copy(d).start()
    scores[h] = score_ref[...]

    def hidden_send(q):
        a_copy(q, 1).wait_recv()
        both = part_ref[:, span(q, h_x)].astype(jnp.float32) + near[q, 1].astype(jnp.float32)
        x_out[q] = both.astype(jnp.bfloat16)
        x_copy(q).start()

    def spread_rows(q):
        a_copy(q, 0).wait_recv()
        both = part_ref[:, span(q, h)].astype(jnp.float32) + near[q, 0].astype(jnp.float32)
        x_copy(q).wait_recv()
        near[q, 0] = (both + x_in[q].astype(jnp.float32)).astype(jnp.bfloat16)
        for zz in range(nz):
            y_out[q, zz] = jnp.dot(
                hot[zz * 2 + 1 - y], near[q, 0], preferred_element_type=jnp.float32
            ).astype(jnp.bfloat16)
            y_copy(q, zz).start()
        for zz in range(nz):
            keep[q, zz] = jnp.dot(hot[zz * 2 + y], near[q, 0], preferred_element_type=jnp.float32)

    def line(q, j):
        @pl.when(z >= j)
        def _():
            @pl.when(z < nz - 1)
            def _():
                if j < nz - 1:
                    dn_copy(q, j + 1).wait_recv()
                    keep[q, z - j] += dn_in[q, j].astype(jnp.float32)
            dn_out[q, j - 1] = keep[q, z - j].astype(jnp.bfloat16)
            dn_copy(q, j).start()

        @pl.when(z <= nz - 1 - j)
        def _():
            @pl.when(z > 0)
            def _():
                if j < nz - 1:
                    up_copy(q, j + 1).wait_recv()
                    keep[q, z + j] += up_in[q, j].astype(jnp.float32)
            up_out[q, j - 1] = keep[q, z + j].astype(jnp.bfloat16)
            up_copy(q, j).start()

    def far(q):
        for zz in range(nz):
            y_copy(q, zz).wait_recv()
            keep[q, zz] += y_in[q, zz].astype(jnp.float32)
        for j in range(nz - 1, 1, -1):
            line(q, j)

    def close(q):
        line(q, 1)

        @pl.when(z < nz - 1)
        def _():
            dn_copy(q, 1).wait_recv()
            keep[q, z] += dn_in[q, 0].astype(jnp.float32)

        @pl.when(z > 0)
        def _():
            up_copy(q, 1).wait_recv()
            keep[q, z] += up_in[q, 0].astype(jnp.float32)

        fin[q] = keep[q, z].astype(jnp.bfloat16)
        for d in range(3):
            f_copy(q, d).start()
        out[:, span(q, h)] = fin[q, pl.ds(pl.multiple_of(h * rows, rows), rows), :]

    hidden_send(0)
    hidden_send(1)

    @pl.loop(0, groups)
    def _(g):
        ids = ids_ref[...] - g * block
        row = lax.broadcasted_iota(jnp.int32, (block, count), 0)
        hot[g] = jnp.where(ids == row, 1.0, 0.0).astype(jnp.bfloat16)

    hidden_send(2)
    hidden_send(3)
    spread_rows(0)
    spread_rows(1)
    far(0)
    spread_rows(2)
    close(0)
    far(1)
    spread_rows(3)
    close(1)
    far(2)
    close(2)
    far(3)
    close(3)

    for d in range(3):
        s_copy(d).wait()
    score_out[...] = scores[0] + scores[1] + scores[2] + scores[3]

    for q in range(BACK):
        for k in range(2):
            a_copy(q, k).wait_send()
        x_copy(q).wait_send()
        for zz in range(nz):
            y_copy(q, zz).wait_send()
        for j in range(1, nz):
            @pl.when(z >= j)
            def _():
                dn_copy(q, j).wait_send()

            @pl.when(z <= nz - 1 - j)
            def _():
                up_copy(q, j).wait_send()
        for d in range(3):
            f_copy(q, d).wait()


def combine(partial_rows, picks, score_part, rows):
    groups = lax.axis_size("expert")
    nz = groups // 2
    count, width = partial_rows.shape
    wide = width // 4 // BACK
    block = 4 * rows
    dma = pltpu.SemaphoreType.DMA
    low = jnp.bfloat16
    vmem = pl.BlockSpec(memory_space=pltpu.VMEM)
    line = pltpu.VMEM((BACK, nz - 1, block, wide), low)
    out, scores = pl.pallas_call(
        functools.partial(combine_kernel, nz),
        out_shape=(
            jax.ShapeDtypeStruct((rows, width), low),
            jax.ShapeDtypeStruct((count // 128, 128), jnp.float32),
        ),
        in_specs=[vmem] * 3,
        out_specs=[vmem] * 2,
        scratch_shapes=[
            pltpu.VMEM((BACK, 2, count, wide), low),
            pltpu.VMEM((BACK, count, wide), low),
            pltpu.VMEM((BACK, count, wide), low),
            pltpu.VMEM((groups, block, count), low),
            pltpu.VMEM((BACK, nz, block, wide), low),
            pltpu.VMEM((BACK, nz, block, wide), low),
            pltpu.VMEM((BACK, nz, block, wide), jnp.float32),
            line, line, line, line,
            pltpu.VMEM((BACK, block, wide), low),
            pltpu.VMEM((4, count // 128, 128), jnp.float32),
            dma((BACK, 2)), dma((BACK, 2)), dma((BACK,)), dma((BACK,)),
            dma((BACK, nz)), dma((BACK, nz)),
            dma((BACK, nz - 1)), dma((BACK, nz - 1)), dma((BACK, nz - 1)), dma((BACK, nz - 1)),
            dma((BACK, 3)), dma((BACK, 3)), dma((3,)), dma((3,)),
        ],
        compiler_params=pltpu.CompilerParams(
            collective_id=1, has_side_effects=True, vmem_limit_bytes=48 * 1024 * 1024),
        name="combine",
    )(partial_rows, picks.reshape(1, count), score_part.reshape(count // 128, 128))
    return out, scores.reshape(score_part.shape)


def local(tokens, grad_out, picks, gates, w_gate, w_up, w_down):
    groups = lax.axis_size("expert")
    shares = lax.axis_size("hidden")
    tok_rows, width = tokens.shape
    exp_local, capacity = picks.shape
    total = groups * shares * tok_rows
    cols = width // shares
    flat = picks.reshape(-1)

    def spread(rows):
        part = lax.all_to_all(rows, "hidden", split_axis=1, concat_axis=0, tiled=True)
        return lax.all_gather(part, "expert", axis=0, tiled=True)

    def collect(everything):
        mine = everything[flat]
        return lax.all_gather(mine, "hidden", axis=1, tiled=True).reshape(exp_local, capacity, width)

    fits = shares == 4 and groups % 2 == 0 and groups == 8 and total * cols <= 4 * 1024 * 1024
    if fits:
        picked, picked_grad = dispatch(tokens, grad_out, picks)
        picked = picked.reshape(exp_local, capacity, width)
        picked_grad = picked_grad.reshape(exp_local, capacity, width)
    else:
        picked_grad = collect(spread(grad_out))
        picked = collect(spread(tokens))
    back = jnp.einsum("xcd,xhd->xch", picked_grad, w_down, preferred_element_type=jnp.float32)
    gate = jnp.einsum("xcd,xhd->xch", picked, w_gate, preferred_element_type=jnp.float32)
    up = jnp.einsum("xcd,xhd->xch", picked, w_up, preferred_element_type=jnp.float32)
    sig = jax.nn.sigmoid(gate)
    act = gate * sig
    hid = (act * up).astype(jnp.bfloat16)
    score_part = jnp.sum(hid.astype(jnp.float32) * back, axis=-1)
    grad_hid = gates[:, :, None] * back
    grad_gate = (grad_hid * up * sig * (1.0 + gate * (1.0 - sig))).astype(jnp.bfloat16)
    grad_up = (grad_hid * act).astype(jnp.bfloat16)
    weighted = (gates[:, :, None] * hid.astype(jnp.float32)).astype(jnp.bfloat16)
    partial_rows = (
        jnp.einsum("xch,xhd->xcd", grad_gate, w_gate, preferred_element_type=jnp.float32)
        + jnp.einsum("xch,xhd->xcd", grad_up, w_up, preferred_element_type=jnp.float32)
    ).astype(jnp.bfloat16)
    if fits:
        grad_tokens, grad_scores = combine(
            partial_rows.reshape(exp_local * capacity, width), picks, score_part, tok_rows
        )
    else:
        grad_scores = lax.psum(score_part, "hidden")
        rows_grad = lax.psum_scatter(
            partial_rows.reshape(exp_local * capacity, width), "hidden", scatter_dimension=1, tiled=True
        )
        selector = (jnp.arange(total, dtype=jnp.int32)[:, None] == flat[None, :]).astype(jnp.bfloat16)
        sums = jnp.dot(selector, rows_grad, preferred_element_type=jnp.float32).astype(jnp.bfloat16)
        own = lax.psum_scatter(sums, "expert", scatter_dimension=0, tiled=True)
        grad_tokens = lax.all_to_all(own, "hidden", split_axis=0, concat_axis=1, tiled=True)
    grad_w_down = jnp.einsum(
        "xch,xcd->xhd", weighted, picked_grad, preferred_element_type=jnp.float32
    ).astype(jnp.bfloat16)
    grad_w_gate = jnp.einsum(
        "xch,xcd->xhd", grad_gate, picked, preferred_element_type=jnp.float32
    ).astype(jnp.bfloat16)
    grad_w_up = jnp.einsum(
        "xch,xcd->xhd", grad_up, picked, preferred_element_type=jnp.float32
    ).astype(jnp.bfloat16)
    return (grad_tokens, grad_scores, grad_w_gate, grad_w_up, grad_w_down)


def solution(mesh):
    placed = (
        P(("expert", "hidden"), None),
        P(("expert", "hidden"), None),
        P("expert", None),
        P("expert", None),
        P("expert", "hidden", None),
        P("expert", "hidden", None),
        P("expert", "hidden", None),
    )
    return jax.shard_map(
        local,
        mesh=mesh,
        in_specs=placed,
        out_specs=(
            P(("expert", "hidden"), None),
            P("expert", None),
            P("expert", "hidden", None),
            P("expert", "hidden", None),
            P("expert", "hidden", None),
        ),
        check_vma=False,
    )
```
